32 devices in a mesh: groups: 2 (over x), rows: 8 (over z, y), rep: 2 (over core).
Axes of the slice: x: 2, y: 2, z: 4, core: 2. Of those that a mesh axis runs over, the one named last changes fastest.
Arguments:
- features: bfloat16 [8192, 256], P(('groups', 'rows')), parts along dimension 0, may hold values from -6 to 6
- weight: bfloat16 [256, 256], replicated, may hold values from -0.375 to 0.375
- tiles: bfloat16 [2048, 128, 128], P(('groups', 'rows', 'rep')), parts along dimension 0, as said below
- tile_place: int32 [128, 16], P(('groups', 'rows', 'rep')), parts along dimension 0, may hold values from 0 to 15, as said below
- panel_count: int32 [128], P(('groups', 'rows', 'rep')), parts along dimension 0, may hold values from 0 to 16, as said below
Outputs:
- diffused: bfloat16 [8192, 256], P(('groups', 'rows', 'rep')), parts along dimension 0
The draws below stay inside these ranges and needn't reach their ends.
There are 2 independent parts, one for each index of `groups`. The reference program is written for one: setup_inputs(seed, part) draws one part's arguments, and reference() takes and returns one part's arrays. A program takes and returns all parts, laid end to end along the dimension named above; an argument that names none is the same for every part. Nothing has to cross between parts.
Inputs may be any that keep to these rules, and one draw needn't show every extreme that they name: `tile_place`: each panel's 16 entries are a permutation of 0 to 15. `panel_count`: slots from the count on are not part of the matrix; in every draw some panel is full and some panel is empty. `tiles`: entries are zero or positive.
All inputs are finite; a program needn't handle non-finite values.
Results may differ from the reference program's by a relative error of at most 0.0065.
Values may be sent and summed in bfloat16 or wider, within the bound.
No kernel may reach another device: no remote copies, remote signals or barrier semaphores. Data moves between devices by JAX's collectives and lax.ppermute only.
A program may use at most 64 MiB of HBM per device.

```python
import math
import jax
import jax.numpy as jnp
from jax import lax

F = 256
TILE = 128
RT = 4
PANEL = 16
SECTIONS = 4
NODES = 4096
N_ROWS = 8
N_REP = 2


def draw_tiles(key, part):
    key = jax.random.fold_in(key, 11)
    key_scale, key_mask, key_value = jax.random.split(key, 3)
    slot_total = N_ROWS * N_REP * SECTIONS * PANEL
    shape = (slot_total, TILE, TILE)
    log_scale = jax.random.uniform(key_scale, (slot_total, 1, 1), jnp.float32, math.log(0.05), math.log(5.0))
    present = jax.random.bernoulli(key_mask, 1.0 / 16.0, shape).astype(jnp.float32)
    values = jax.random.uniform(key_value, shape, jnp.float32, 0.5, 1.5)
    return (jnp.exp(log_scale) * present * values).astype(jnp.bfloat16)


def draw_tile_place(key, part):
    key = jax.random.fold_in(key, 12)
    panel_total = N_ROWS * N_REP * SECTIONS
    scores = jax.random.randint(key, (panel_total, PANEL), 0, 1048576) * PANEL + jnp.arange(PANEL, dtype=jnp.int32)[None, :]
    return jnp.argsort(scores, axis=1, stable=True).astype(jnp.int32)


def draw_panel_count(key, part):
    key = jax.random.fold_in(key, 13)
    key_level, key_count, key_full, key_empty = jax.random.split(key, 4)
    device_total = N_ROWS * N_REP
    panel_total = device_total * SECTIONS
    levels = jax.random.randint(key_level, (device_total,), 0, 4)
    ceiling = jnp.maximum(PANEL // jnp.left_shift(1, levels), 1)
    ceiling = jnp.repeat(ceiling, SECTIONS)
    counts = jax.random.randint(key_count, (panel_total,), 0, ceiling + 1)
    full_panel = jax.random.randint(key_full, (), 0, panel_total)
    empty_panel = (full_panel + 1 + jax.random.randint(key_empty, (), 0, panel_total - 1)) % panel_total
    counts = counts.at[full_panel].set(PANEL)
    counts = counts.at[empty_panel].set(0)
    return counts.astype(jnp.int32)


def steps_of(key, shape, cuts, low, high):
    factor_of, own = 1.0, jax.random.fold_in(key, 6)
    for position, blocks in cuts:
        steps = jnp.exp(jax.random.uniform(jax.random.fold_in(own, position), (blocks,), jnp.float32, low / len(cuts), high / len(cuts)))
        factor_of = factor_of * jnp.repeat(steps, shape[position] // blocks).reshape([-1 if axis == position else 1 for axis in range(len(shape))])
    return factor_of


def normal_values(rng, dims, scale, bound, cuts=(), kind=jnp.bfloat16):
    factor_of = steps_of(rng, dims, cuts, -0.22, 0.18) if cuts else 1.0
    result = jax.random.normal(rng, dims, jnp.float32) * scale * factor_of
    return jnp.minimum(jnp.maximum(result, -bound), bound).astype(kind)


def setup_inputs(seed: int = 0, part: int = 0) -> dict:
    seeds = jax.random.split(jax.random.key(seed), 6)
    part_splits = jax.random.split(jax.random.fold_in(seeds[5], part), 6)
    features = normal_values(part_splits[0], (NODES, F), 1.0, 6.0, ((0, 8),))
    weight = normal_values(seeds[1], (F, F), F ** -0.5, 0.375)
    tiles = draw_tiles(jax.random.fold_in(jax.random.fold_in(seeds[5], part), 71), part)
    tile_place = draw_tile_place(jax.random.fold_in(jax.random.fold_in(seeds[5], part), 71), part)
    panel_count = draw_panel_count(jax.random.fold_in(jax.random.fold_in(seeds[5], part), 71), part)
    return dict(features=features, weight=weight, tiles=tiles, tile_place=tile_place, panel_count=panel_count)


def reference(features, weight, tiles, tile_place, panel_count):
    panel_total = N_ROWS * N_REP * SECTIONS
    slot_index = jnp.arange(panel_total * PANEL, dtype=jnp.int32)
    panel_index = slot_index // PANEL
    slot_inner = slot_index % PANEL
    device_index = panel_index // SECTIONS
    section_index = panel_index % SECTIONS
    row_block = device_index // N_REP
    replica = device_index % N_REP
    column_block = (row_block - replica - N_REP * section_index) % N_ROWS
    places = tile_place.reshape(-1).astype(jnp.int32)
    is_alive = slot_inner < panel_count[panel_index]
    out_tile = (row_block * RT + places // RT).astype(jnp.int32)
    in_tile = (column_block * RT + places % RT).astype(jnp.int32)
    tile_rows = NODES // TILE
    row_sums = lax.optimization_barrier(jnp.sum(tiles, axis=2, dtype=jnp.float32)) * is_alive[:, None].astype(jnp.float32)
    degree = 1.0 + jnp.zeros((tile_rows, TILE), jnp.float32).at[out_tile].add(row_sums).reshape(NODES)
    scale = lax.rsqrt(degree)
    ordering = jnp.argsort(1 - is_alive.astype(jnp.int32), stable=True).astype(jnp.int32)
    block_slots = PANEL * N_REP
    ordered_blocks = ordering.reshape(-1, block_slots)

    def spread(field):
        field_tiles = field.reshape(tile_rows, TILE, F)

        def visit(summed, chosen):

            def add_block(acc):
                squares = tiles[chosen].astype(jnp.float32)
                inputs = field_tiles[in_tile[chosen]].astype(jnp.float32)
                products = jnp.einsum('kij,kjf->kif', squares, inputs)
                products = products * is_alive[chosen][:, None, None].astype(jnp.float32)
                return acc.at[out_tile[chosen]].add(products)
            return (lax.cond(jnp.any(is_alive[chosen]), add_block, lambda acc: acc, summed), None)
        summed, unused = lax.scan(visit, jnp.zeros((tile_rows, TILE, F), jnp.float32), ordered_blocks)
        return summed.reshape(NODES, F)
    first = (scale[:, None] * features.astype(jnp.float32)).astype(jnp.bfloat16)
    first_image = spread(first)
    heat_one = scale[:, None] * (first_image + first.astype(jnp.float32))
    second = (scale[:, None] * heat_one).astype(jnp.bfloat16)
    second_image = spread(second)
    heat_two = scale[:, None] * (second_image + second.astype(jnp.float32))
    mixed = (features.astype(jnp.float32) + 5.0 * heat_one + 12.5 * heat_two).astype(jnp.bfloat16)
    return jnp.dot(mixed, weight, preferred_element_type=jnp.float32).astype(jnp.bfloat16)
```

```python
import functools

import jax
import jax.numpy as jnp
from jax import lax
from jax.experimental import pallas as pl
from jax.experimental.pallas import tpu as pltpu
from jax.sharding import PartitionSpec as P

F32 = jnp.float32
BF16 = jnp.bfloat16
VMEM = pl.BlockSpec(memory_space=pltpu.VMEM)
SMEM = pl.BlockSpec(memory_space=pltpu.SMEM)
ANY = pl.BlockSpec(memory_space=pl.ANY)
PARAMS = pltpu.CompilerParams(vmem_limit_bytes=56 * 2**20)


def xor_permute(block, axis, distance):
    return lax.ppermute(block, axis, [(i, i ^ distance) for i in range(lax.axis_size(axis))])


def gathered(block, axis, size):
    if size == 1:
        return [block]
    if size == 2:
        return [block, xor_permute(block, axis, 1)]
    half = size // 2
    far = xor_permute(block, axis, half)
    near = gathered(block, axis, half)
    return near + [far] + [xor_permute(far, axis, d) for d in range(1, half)]


def swapped(block, axis):
    return lax.ppermute(block, axis, [(0, 1), (1, 0)])


def place_kernel(place_ref, count_ref, tiles_ref, dense_ref, degree_ref, sems):
    section_total, slot_total = place_ref.shape
    rows_here = dense_ref.shape[1]
    tile_dim = tiles_ref.shape[1]
    tile_span = rows_here // tile_dim

    def spot(s, k):
        place = place_ref[s, k]
        row = pl.multiple_of((place // tile_span) * tile_dim, tile_dim)
        col = pl.multiple_of((place % tile_span) * tile_dim, tile_dim)
        return dense_ref.at[s, pl.ds(row, tile_dim), pl.ds(col, tile_dim)]

    def copy(s, k):
        slot = s * slot_total + k
        return pltpu.make_async_copy(tiles_ref.at[slot], spot(s, k), sems.at[slot])

    def place_section(s, carry):
        for k in range(slot_total):

            @pl.when(k < count_ref[s])
            def _():
                copy(s, k).start()

            @pl.when(k >= count_ref[s])
            def _():
                spot(s, k)[...] = jnp.zeros((tile_dim, tile_dim), BF16)

        return carry

    lax.fori_loop(0, section_total, place_section, 0)
    degree_ref[...] = jnp.zeros_like(degree_ref)
    ones = jnp.ones((rows_here, degree_ref.shape[1]), BF16)

    def sum_section(s, carry):
        for k in range(slot_total):

            @pl.when(k < count_ref[s])
            def _():
                copy(s, k).wait()

        degree_ref[...] += jnp.dot(dense_ref[s], ones, preferred_element_type=F32)
        return carry

    lax.fori_loop(0, section_total, sum_section, 0)


def image(index_ref, own_ref, other_ref, block_refs, held):
    for d, block_ref in enumerate(block_refs):
        held[d] = block_ref[...]
    total = held[0].astype(F32)
    for core, dense_ref in enumerate((own_ref, other_ref)):
        for s in range(dense_ref.shape[0]):
            total += jnp.dot(
                dense_ref[s], held[index_ref[core, s]], preferred_element_type=F32
            )
    return total


def first_kernel(block_total, index_ref, own_ref, other_ref, scale_ref, *refs):
    block_refs = refs[:block_total]
    heat_ref, second_ref, held = refs[block_total:]
    scale = scale_ref[...]
    heat = scale * image(index_ref, own_ref, other_ref, block_refs, held)
    heat_ref[...] = heat
    second_ref[...] = (scale * heat).astype(BF16)


def second_kernel(
    block_total, index_ref, replica_ref, own_ref, other_ref, scale_ref, heat_ref, feature_ref, *refs
):
    block_refs = refs[:block_total]
    keep_ref, send_ref, held, mixed = refs[block_total:]
    heat_two = scale_ref[...] * image(index_ref, own_ref, other_ref, block_refs, held)
    mixed[...] = (
        feature_ref[...].astype(F32) + 5.0 * heat_ref[...] + 12.5 * heat_two
    ).astype(BF16)
    half = keep_ref.shape[0]
    replica = replica_ref[0]
    keep_ref[...] = mixed[pl.ds(pl.multiple_of(replica * half, half), half), :]
    send_ref[...] = mixed[pl.ds(pl.multiple_of((1 - replica) * half, half), half), :]


def per_device(features, weight, tiles, tile_place, panel_count):
    rows_here, width = features.shape
    section_total = panel_count.shape[0]
    row_total = lax.axis_size("rows")
    rep_total = lax.axis_size("rep")
    row_index = lax.axis_index("rows")
    replica = lax.axis_index("rep")
    half_rows = rows_here // rep_total
    part = width // rep_total
    shape = jax.ShapeDtypeStruct

    dense, degree = pl.pallas_call(
        place_kernel,
        out_shape=(
            shape((section_total, rows_here, rows_here), BF16),
            shape((rows_here, part), F32),
        ),
        in_specs=[SMEM, SMEM, ANY],
        out_specs=(VMEM, VMEM),
        scratch_shapes=[pltpu.SemaphoreType.DMA((tiles.shape[0],))],
        compiler_params=PARAMS,
    )(tile_place, panel_count, tiles)
    scale = lax.rsqrt(1.0 + (degree + swapped(degree, "rep")))
    features_part = lax.dynamic_slice_in_dim(features, replica * part, part, 1)
    first = (scale * features_part).astype(BF16)
    dense_other = swapped(dense, "rep")

    cores = jnp.stack([replica, 1 - replica])[:, None]
    steps = cores + rep_total * jnp.arange(section_total)[None, :]
    index = (row_index ^ ((row_index - steps) % row_total)).astype(jnp.int32)

    blocks = gathered(first, "rows", row_total)
    held = pltpu.VMEM((row_total, rows_here, part), BF16)
    heat_one, second = pl.pallas_call(
        functools.partial(first_kernel, row_total),
        out_shape=(shape((rows_here, part), F32), shape((rows_here, part), BF16)),
        in_specs=[SMEM] + [VMEM] * (3 + row_total),
        out_specs=(VMEM, VMEM),
        scratch_shapes=[held],
        compiler_params=PARAMS,
    )(index, dense, dense_other, scale, *blocks)

    blocks = gathered(second, "rows", row_total)
    keep, send = pl.pallas_call(
        functools.partial(second_kernel, row_total),
        out_shape=(shape((half_rows, part), BF16),) * 2,
        in_specs=[SMEM, SMEM] + [VMEM] * (5 + row_total),
        out_specs=(VMEM, VMEM),
        scratch_shapes=[held, pltpu.VMEM((rows_here, part), BF16)],
        compiler_params=PARAMS,
    )(index, replica.reshape(1), dense, dense_other, scale, heat_one, features_part, *blocks)
    got = swapped(send, "rep")
    weight_own = lax.dynamic_slice_in_dim(weight, replica * part, part, 0)
    weight_other = lax.dynamic_slice_in_dim(weight, (1 - replica) * part, part, 0)
    return (
        jnp.dot(keep, weight_own, preferred_element_type=F32)
        + jnp.dot(got, weight_other, preferred_element_type=F32)
    ).astype(BF16)


def solution(mesh):
    in_specs = (
        P(("groups", "rows"), None),
        P(),
        P(("groups", "rows", "rep"), None, None),
        P(("groups", "rows", "rep"), None),
        P(("groups", "rows", "rep")),
    )
    out_specs = P(("groups", "rows", "rep"), None)
    return jax.shard_map(
        per_device, mesh=mesh, in_specs=in_specs, out_specs=out_specs, check_vma=False
    )
```

```python
import functools
import math

import jax
import jax.numpy as jnp
from jax import lax
from jax.experimental import pallas as pl
from jax.experimental.pallas import tpu as pltpu
from jax.sharding import PartitionSpec as P

F32 = jnp.float32
BF16 = jnp.bfloat16
VMEM = pl.BlockSpec(memory_space=pltpu.VMEM)
HBM = pl.BlockSpec(memory_space=pltpu.HBM)


def params(*arrays):
    held = sum(math.prod(shape) * jnp.dtype(kind).itemsize for shape, kind in arrays)
    return pltpu.CompilerParams(vmem_limit_bytes=held + 6 * 2**20)


def in_vmem(block):
    return pltpu.with_memory_space_constraint(block, pltpu.VMEM)


def in_hbm(block):
    return pltpu.with_memory_space_constraint(block, pltpu.HBM)


def xor_permute(block, axis, distance):
    return lax.ppermute(block, axis, [(i, i ^ distance) for i in range(lax.axis_size(axis))])


def gathered(block, axis, size):
    if size == 1:
        return [block]
    if size == 2:
        return [block, xor_permute(block, axis, 1)]
    half = size // 2
    near = gathered(block, axis, half)
    far = xor_permute(block, axis, half)
    far, *near = lax.optimization_barrier((far, *near))
    return near + [far] + [xor_permute(far, axis, d) for d in range(1, half)]


def swapped(block, axis):
    return lax.ppermute(block, axis, [(0, 1), (1, 0)])


def place_kernel(
    place_hbm, count_hbm, tiles_ref, dense_ref, degree_ref, held, place_ref, count_ref, sems
):
    section_total, slot_total = place_ref.shape
    rows_here = dense_ref.shape[1]
    tile_dim = tiles_ref.shape[1]
    tile_span = rows_here // tile_dim

    def copy(s):
        slots = pl.ds(s * slot_total, slot_total)
        return pltpu.make_async_copy(tiles_ref.at[slots], held.at[slots], sems.at[s])

    places = pltpu.make_async_copy(place_hbm, place_ref, sems.at[section_total])
    counts = pltpu.make_async_copy(count_hbm, count_ref, sems.at[section_total + 1])
    places.start()
    counts.start()
    for s in range(section_total):
        copy(s).start()
    places.wait()
    counts.wait()
    ones = jnp.ones((rows_here, degree_ref.shape[1]), BF16)
    for s in range(section_total):
        copy(s).wait()
        for k in range(slot_total):
            place = place_ref[s, k]
            row = pl.multiple_of((place // tile_span) * tile_dim, tile_dim)
            col = pl.multiple_of((place % tile_span) * tile_dim, tile_dim)
            tile = held[s * slot_total + k]
            dense_ref[s, pl.ds(row, tile_dim), pl.ds(col, tile_dim)] = jnp.where(
                k < count_ref[s], tile, jnp.zeros_like(tile)
            )
        sums = jnp.dot(dense_ref[s], ones, preferred_element_type=F32)
        if s == 0:
            degree_ref[...] = sums
        else:
            degree_ref[...] += sums


def part_of(ref, index, size):
    return ref[:, pl.ds(pl.multiple_of(index * size, size), size)]


def scale_kernel(degree_ref, other_ref, feature_ref, scale_ref, first_ref):
    scale = lax.rsqrt(1.0 + (degree_ref[...] + other_ref[...]))
    scale_ref[...] = scale
    feature = part_of(feature_ref, lax.axis_index("rep"), scale.shape[1])
    first_ref[...] = (scale * feature.astype(F32)).astype(BF16)


def image(own_ref, other_ref, block_refs, held, finish, chunk=256):
    row_total = len(block_refs)
    rep_total = row_total // own_ref.shape[0]
    row_index = lax.axis_index("rows")
    replica = lax.axis_index("rep")
    for d, block_ref in enumerate(block_refs):
        held[d] = block_ref[...]
    for low in range(0, own_ref.shape[1], chunk):
        rows = pl.ds(low, chunk)
        total = held[0, rows].astype(F32)
        for dense_ref, core in ((own_ref, replica), (other_ref, 1 - replica)):
            for s in range(dense_ref.shape[0]):
                column = lax.rem(row_index - core - rep_total * s + row_total, row_total)
                total += jnp.dot(
                    dense_ref[s, rows], held[row_index ^ column], preferred_element_type=F32
                )
        finish(rows, total)


def first_kernel(own_ref, other_ref, scale_ref, *refs):
    *block_refs, heat_ref, second_ref, held = refs

    def finish(rows, total):
        scale = scale_ref[rows]
        heat = scale * total
        heat_ref[rows] = heat
        second_ref[rows] = (scale * heat).astype(BF16)

    image(own_ref, other_ref, block_refs, held, finish)


def second_kernel(own_ref, other_ref, scale_ref, heat_ref, feature_ref, *refs):
    *block_refs, keep_ref, send_ref, held, mixed = refs
    replica = lax.axis_index("rep")
    part = mixed.shape[1]

    def finish(rows, total):
        feature = feature_ref[rows, pl.ds(pl.multiple_of(replica * part, part), part)]
        heat_two = scale_ref[rows] * total
        mixed[rows] = (feature.astype(F32) + 5.0 * heat_ref[rows] + 12.5 * heat_two).astype(BF16)

    image(own_ref, other_ref, block_refs, held, finish)
    half = keep_ref.shape[0]
    keep_ref[...] = mixed[pl.ds(pl.multiple_of(replica * half, half), half), :]
    send_ref[...] = mixed[pl.ds(pl.multiple_of((1 - replica) * half, half), half), :]


def project_kernel(keep_ref, got_ref, weight_ref, out_ref):
    replica = lax.axis_index("rep")
    part = keep_ref.shape[1]
    total = 0.0
    for mixed_ref, core in ((keep_ref, replica), (got_ref, 1 - replica)):
        weight = weight_ref[pl.ds(pl.multiple_of(core * part, part), part), :]
        total += jnp.dot(mixed_ref[...], weight, preferred_element_type=F32)
    out_ref[...] = total.astype(BF16)


def per_device(features, weight, tiles, tile_place, panel_count):
    rows_here, width = features.shape
    section_total = panel_count.shape[0]
    row_total = lax.axis_size("rows")
    rep_total = lax.axis_size("rep")
    half_rows = rows_here // rep_total
    part = width // rep_total
    shape = pltpu.VMEM
    panels = (section_total, rows_here, rows_here), BF16
    column = (rows_here, part), F32
    field = (rows_here, part), BF16
    held = (row_total, rows_here, part), BF16
    half = (half_rows, part), BF16

    dense, degree = pl.pallas_call(
        place_kernel,
        out_shape=(shape(*panels), shape(*column)),
        in_specs=[HBM, HBM, HBM],
        out_specs=(VMEM, VMEM),
        scratch_shapes=[
            pltpu.VMEM(tiles.shape, BF16),
            pltpu.SMEM(tile_place.shape, jnp.int32),
            pltpu.SMEM(panel_count.shape, jnp.int32),
            pltpu.SemaphoreType.DMA((section_total + 2,)),
        ],
        compiler_params=params(panels, panels, column),
    )(in_hbm(tile_place), in_hbm(panel_count), in_hbm(tiles))
    degree_other = swapped(degree, "rep")
    scale, first = pl.pallas_call(
        scale_kernel,
        out_shape=(shape(*column), shape(*field)),
        in_specs=[VMEM] * 3,
        out_specs=(VMEM, VMEM),
        compiler_params=params(column, column, column, column),
    )(degree, degree_other, features)

    blocks = gathered(first, "rows", row_total)
    dense_late, blocks[1] = lax.optimization_barrier((dense, blocks[1]))
    dense_other = in_vmem(swapped(dense_late, "rep"))
    heat_one, second = pl.pallas_call(
        first_kernel,
        out_shape=(shape(*column), shape(*field)),
        in_specs=[VMEM] * (3 + row_total),
        out_specs=(VMEM, VMEM),
        scratch_shapes=[pltpu.VMEM(*held)],
        compiler_params=params(panels, panels, column, column, held, held),
    )(dense, dense_other, scale, *blocks)

    blocks = gathered(second, "rows", row_total)
    keep, send = pl.pallas_call(
        second_kernel,
        out_shape=(shape(*half), shape(*half)),
        in_specs=[VMEM] * (5 + row_total),
        out_specs=(VMEM, VMEM),
        scratch_shapes=[pltpu.VMEM(*held), pltpu.VMEM(*field)],
        compiler_params=params(panels, panels, column, column, column, held, held),
    )(dense, dense_other, scale, heat_one, features, *blocks)
    got = swapped(send, "rep")
    return pl.pallas_call(
        project_kernel,
        out_shape=jax.ShapeDtypeStruct((half_rows, width), BF16),
        in_specs=[VMEM] * 3,
        out_specs=VMEM,
        compiler_params=params(column, column),
    )(keep, got, in_vmem(weight))


def solution(mesh):
    in_specs = (
        P(("groups", "rows"), None),
        P(),
        P(("groups", "rows", "rep"), None, None),
        P(("groups", "rows", "rep"), None),
        P(("groups", "rows", "rep")),
    )
    out_specs = P(("groups", "rows", "rep"), None)
    return jax.shard_map(
        per_device, mesh=mesh, in_specs=in_specs, out_specs=out_specs, check_vma=False
    )
```

```python
import functools
import math

import jax
import jax.numpy as jnp
from jax import lax
from jax.experimental import pallas as pl
from jax.experimental.pallas import tpu as pltpu
from jax.sharding import PartitionSpec as P

F32 = jnp.float32
BF16 = jnp.bfloat16
VMEM = pl.BlockSpec(memory_space=pltpu.VMEM)
HBM = pl.BlockSpec(memory_space=pltpu.HBM)


def params(*arrays):
    held = sum(math.prod(shape) * jnp.dtype(kind).itemsize for shape, kind in arrays)
    return pltpu.CompilerParams(vmem_limit_bytes=held + 6 * 2**20)


def in_vmem(block):
    return pltpu.with_memory_space_constraint(block, pltpu.VMEM)


def in_hbm(block):
    return pltpu.with_memory_space_constraint(block, pltpu.HBM)


def xor_permute(block, axis, distance):
    return lax.ppermute(block, axis, [(i, i ^ distance) for i in range(lax.axis_size(axis))])


def gathered(block, axis, size):
    if size == 1:
        return [block]
    half = size // 2
    far = xor_permute(block, axis, half)
    near = [xor_permute(block, axis, d) for d in range(half - 1, 0, -1)]
    far_near = [xor_permute(far, axis, d) for d in range(half - 1, 0, -1)]
    return [block, *near[::-1], far, *far_near[::-1]]


def swapped(block, axis):
    return lax.ppermute(block, axis, [(0, 1), (1, 0)])


def place_kernel(
    place_hbm, count_hbm, tiles_ref, dense_ref, degree_ref, held, place_ref, count_ref, sems
):
    section_total, slot_total = place_ref.shape
    rows_here = dense_ref.shape[1]
    tile_dim = tiles_ref.shape[1]
    tile_span = rows_here // tile_dim

    def copy(s):
        slots = pl.ds(s * slot_total, slot_total)
        return pltpu.make_async_copy(tiles_ref.at[slots], held.at[slots], sems.at[s])

    places = pltpu.make_async_copy(place_hbm, place_ref, sems.at[section_total])
    counts = pltpu.make_async_copy(count_hbm, count_ref, sems.at[section_total + 1])
    places.start()
    counts.start()
    for s in range(section_total):
        copy(s).start()
    places.wait()
    counts.wait()
    ones = jnp.ones((rows_here, degree_ref.shape[1]), BF16)
    for s in range(section_total):
        copy(s).wait()
        for k in range(slot_total):
            place = place_ref[s, k]
            row = pl.multiple_of((place // tile_span) * tile_dim, tile_dim)
            col = pl.multiple_of((place % tile_span) * tile_dim, tile_dim)
            tile = held[s * slot_total + k]
            dense_ref[s, pl.ds(row, tile_dim), pl.ds(col, tile_dim)] = jnp.where(
                k < count_ref[s], tile, jnp.zeros_like(tile)
            )
        sums = jnp.dot(dense_ref[s], ones, preferred_element_type=F32)
        if s == 0:
            degree_ref[...] = sums
        else:
            degree_ref[...] += sums


def part_of(ref, index, size):
    return ref[:, pl.ds(pl.multiple_of(index * size, size), size)]


def scale_kernel(degree_ref, other_ref, feature_ref, scale_ref, first_ref):
    scale = lax.rsqrt(1.0 + (degree_ref[...] + other_ref[...]))
    scale_ref[...] = scale
    feature = part_of(feature_ref, lax.axis_index("rep"), scale.shape[1])
    first_ref[...] = (scale * feature.astype(F32)).astype(BF16)


def image(own_ref, other_ref, block_refs, held, finish, chunk=256):
    row_total = len(block_refs)
    rep_total = row_total // own_ref.shape[0]
    row_index = lax.axis_index("rows")
    replica = lax.axis_index("rep")
    for d, block_ref in enumerate(block_refs):
        held[d] = block_ref[...]
    for low in range(0, own_ref.shape[1], chunk):
        rows = pl.ds(low, chunk)
        total = held[0, rows].astype(F32)
        for dense_ref, core in ((own_ref, replica), (other_ref, 1 - replica)):
            for s in range(dense_ref.shape[0]):
                column = lax.rem(row_index - core - rep_total * s + row_total, row_total)
                total += jnp.dot(
                    dense_ref[s, rows], held[row_index ^ column], preferred_element_type=F32
                )
        finish(rows, total)


def first_kernel(own_ref, other_ref, scale_ref, *refs):
    *block_refs, heat_ref, second_ref, held = refs

    def finish(rows, total):
        scale = scale_ref[rows]
        heat = scale * total
        heat_ref[rows] = heat
        second_ref[rows] = (scale * heat).astype(BF16)

    image(own_ref, other_ref, block_refs, held, finish)


def second_kernel(own_ref, other_ref, scale_ref, heat_ref, feature_ref, *refs):
    *block_refs, keep_ref, send_ref, held, mixed = refs
    replica = lax.axis_index("rep")
    part = mixed.shape[1]

    def finish(rows, total):
        feature = feature_ref[rows, pl.ds(pl.multiple_of(replica * part, part), part)]
        heat_two = scale_ref[rows] * total
        mixed[rows] = (feature.astype(F32) + 5.0 * heat_ref[rows] + 12.5 * heat_two).astype(BF16)

    image(own_ref, other_ref, block_refs, held, finish)
    half = keep_ref.shape[0]
    keep_ref[...] = mixed[pl.ds(pl.multiple_of(replica * half, half), half), :]
    send_ref[...] = mixed[pl.ds(pl.multiple_of((1 - replica) * half, half), half), :]


def project_kernel(keep_ref, got_ref, weight_ref, out_ref):
    replica = lax.axis_index("rep")
    part = keep_ref.shape[1]
    total = 0.0
    for mixed_ref, core in ((keep_ref, replica), (got_ref, 1 - replica)):
        weight = weight_ref[pl.ds(pl.multiple_of(core * part, part), part), :]
        total += jnp.dot(mixed_ref[...], weight, preferred_element_type=F32)
    out_ref[...] = total.astype(BF16)


def per_device(features, weight, tiles, tile_place, panel_count):
    rows_here, width = features.shape
    section_total = panel_count.shape[0]
    row_total = lax.axis_size("rows")
    rep_total = lax.axis_size("rep")
    half_rows = rows_here // rep_total
    part = width // rep_total
    shape = pltpu.VMEM
    panels = (section_total, rows_here, rows_here), BF16
    column = (rows_here, part), F32
    field = (rows_here, part), BF16
    held = (row_total, rows_here, part), BF16
    half = (half_rows, part), BF16

    dense, degree = pl.pallas_call(
        place_kernel,
        out_shape=(shape(*panels), shape(*column)),
        in_specs=[HBM, HBM, HBM],
        out_specs=(VMEM, VMEM),
        scratch_shapes=[
            pltpu.VMEM(tiles.shape, BF16),
            pltpu.SMEM(tile_place.shape, jnp.int32),
            pltpu.SMEM(panel_count.shape, jnp.int32),
            pltpu.SemaphoreType.DMA((section_total + 2,)),
        ],
        compiler_params=params(panels, panels, column),
    )(in_hbm(tile_place), in_hbm(panel_count), in_hbm(tiles))
    degree_other = swapped(degree, "rep")
    scale, first = pl.pallas_call(
        scale_kernel,
        out_shape=(shape(*column), shape(*field)),
        in_specs=[VMEM] * 3,
        out_specs=(VMEM, VMEM),
        compiler_params=params(column, column, column, column),
    )(degree, degree_other, features)

    blocks = gathered(first, "rows", row_total)
    dense_late, _ = lax.optimization_barrier((dense, scale))
    dense_other = in_vmem(swapped(dense_late, "rep"))
    heat_one, second = pl.pallas_call(
        first_kernel,
        out_shape=(shape(*column), shape(*field)),
        in_specs=[VMEM] * (3 + row_total),
        out_specs=(VMEM, VMEM),
        scratch_shapes=[pltpu.VMEM(*held)],
        compiler_params=params(panels, panels, column, column, held, held),
    )(dense, dense_other, scale, *blocks)

    blocks = gathered(second, "rows", row_total)
    keep, send = pl.pallas_call(
        second_kernel,
        out_shape=(shape(*half), shape(*half)),
        in_specs=[VMEM] * (5 + row_total),
        out_specs=(VMEM, VMEM),
        scratch_shapes=[pltpu.VMEM(*held), pltpu.VMEM(*field)],
        compiler_params=params(panels, panels, column, column, column, held, held),
    )(dense, dense_other, scale, heat_one, features, *blocks)
    got = swapped(send, "rep")
    return pl.pallas_call(
        project_kernel,
        out_shape=jax.ShapeDtypeStruct((half_rows, width), BF16),
        in_specs=[VMEM] * 3,
        out_specs=VMEM,
        compiler_params=params(column, column),
    )(keep, got, in_vmem(weight))


def solution(mesh):
    in_specs = (
        P(("groups", "rows"), None),
        P(),
        P(("groups", "rows", "rep"), None, None),
        P(("groups", "rows", "rep"), None),
        P(("groups", "rows", "rep")),
    )
    out_specs = P(("groups", "rows", "rep"), None)
    return jax.shard_map(
        per_device, mesh=mesh, in_specs=in_specs, out_specs=out_specs, check_vma=False
    )
```

```python
import functools
import math

import jax
import jax.numpy as jnp
from jax import lax
from jax.experimental import pallas as pl
from jax.experimental.pallas import tpu as pltpu
from jax.sharding import PartitionSpec as P

F32 = jnp.float32
BF16 = jnp.bfloat16
VMEM = pl.BlockSpec(memory_space=pltpu.VMEM)
HBM = pl.BlockSpec(memory_space=pltpu.HBM)


def params(*arrays):
    held = sum(math.prod(shape) * jnp.dtype(kind).itemsize for shape, kind in arrays)
    return pltpu.CompilerParams(vmem_limit_bytes=held + 6 * 2**20)


def in_vmem(block):
    return pltpu.with_memory_space_constraint(block, pltpu.VMEM)


def in_hbm(block):
    return pltpu.with_memory_space_constraint(block, pltpu.HBM)


def xor_permute(block, axis, distance):
    return lax.ppermute(block, axis, [(i, i ^ distance) for i in range(lax.axis_size(axis))])


def gathered(block, axis, size, also=None):
    half = size // 2
    blocks = {0: block}
    for d in [1, half, *range(2, half)]:
        blocks[d] = xor_permute(block, axis, d)
    early = [half, *range(1, half - 1)]
    tied, also = lax.optimization_barrier(([blocks[d] for d in early], also))
    blocks.update(zip(early, tied))
    for d in range(half - 1, 0, -1):
        blocks[half + d] = xor_permute(blocks[half], axis, d)
    return [blocks[d] for d in range(size)], also


def swapped(block, axis):
    return lax.ppermute(block, axis, [(0, 1), (1, 0)])


def place_kernel(
    place_hbm, count_hbm, tiles_ref, dense_ref, degree_ref, held, place_ref, count_ref, sems
):
    section_total, slot_total = place_ref.shape
    rows_here = dense_ref.shape[1]
    tile_dim = tiles_ref.shape[1]
    tile_span = rows_here // tile_dim

    def copy(s):
        slots = pl.ds(s * slot_total, slot_total)
        return pltpu.make_async_copy(tiles_ref.at[slots], held.at[slots], sems.at[s])

    places = pltpu.make_async_copy(place_hbm, place_ref, sems.at[section_total])
    counts = pltpu.make_async_copy(count_hbm, count_ref, sems.at[section_total + 1])
    places.start()
    counts.start()
    for s in range(section_total):
        copy(s).start()
    places.wait()
    counts.wait()
    ones = jnp.ones((rows_here, degree_ref.shape[1]), BF16)
    for s in range(section_total):
        copy(s).wait()
        for k in range(slot_total):
            place = place_ref[s, k]
            row = pl.multiple_of((place // tile_span) * tile_dim, tile_dim)
            col = pl.multiple_of((place % tile_span) * tile_dim, tile_dim)
            tile = held[s * slot_total + k]
            dense_ref[s, pl.ds(row, tile_dim), pl.ds(col, tile_dim)] = jnp.where(
                k < count_ref[s], tile, jnp.zeros_like(tile)
            )
        sums = jnp.dot(dense_ref[s], ones, preferred_element_type=F32)
        if s == 0:
            degree_ref[...] = sums
        else:
            degree_ref[...] += sums


def part_of(ref, index, size):
    return ref[:, pl.ds(pl.multiple_of(index * size, size), size)]


def scale_kernel(degree_ref, other_ref, feature_ref, scale_ref, first_ref):
    scale = lax.rsqrt(1.0 + (degree_ref[...] + other_ref[...]))
    scale_ref[...] = scale
    feature = part_of(feature_ref, lax.axis_index("rep"), scale.shape[1])
    first_ref[...] = (scale * feature.astype(F32)).astype(BF16)


def add_image(far, row_total, own_ref, other_ref, block_refs, held, start, finish, chunk=256):
    rep_total = row_total // own_ref.shape[0]
    row_index = lax.axis_index("rows")
    replica = lax.axis_index("rep")
    for i, block_ref in enumerate(block_refs):
        held[i] = block_ref[...]
    for first_row in range(0, own_ref.shape[1], chunk):
        rows = pl.ds(first_row, chunk)
        total = start(rows)
        for i in range(0, len(block_refs), rep_total):
            for dense_ref, core in ((own_ref, replica), (other_ref, 1 - replica)):
                column = row_index ^ (far[i] + core * (far[i + 1] - far[i]))
                section = lax.rem(row_index - column + row_total, row_total) // rep_total
                total += jnp.dot(
                    dense_ref[section, rows], held[i + core], preferred_element_type=F32
                )
        finish(rows, total)


def near_kernel(far, row_total, own_ref, other_ref, *refs):
    *block_refs, total_ref, held = refs

    def start(rows):
        return block_refs[0][rows].astype(F32)

    def finish(rows, total):
        total_ref[rows] = total

    add_image(far, row_total, own_ref, other_ref, block_refs, held, start, finish)


def more_kernel(far, row_total, own_ref, other_ref, sum_ref, *refs):
    *block_refs, total_ref, held = refs

    def finish(rows, total):
        total_ref[rows] = total

    add_image(far, row_total, own_ref, other_ref, block_refs, held, lambda rows: sum_ref[rows], finish)


def first_kernel(far, row_total, own_ref, other_ref, sum_ref, scale_ref, *refs):
    *block_refs, heat_ref, second_ref, held = refs

    def finish(rows, total):
        scale = scale_ref[rows]
        heat = scale * total
        heat_ref[rows] = heat
        second_ref[rows] = (scale * heat).astype(BF16)

    add_image(far, row_total, own_ref, other_ref, block_refs, held, lambda rows: sum_ref[rows], finish)


def second_kernel(
    far, row_total, own_ref, other_ref, sum_ref, scale_ref, heat_ref, feature_ref, *refs
):
    *block_refs, keep_ref, send_ref, held, mixed = refs
    replica = lax.axis_index("rep")
    part = mixed.shape[1]

    def finish(rows, total):
        feature = feature_ref[rows, pl.ds(pl.multiple_of(replica * part, part), part)]
        heat_two = scale_ref[rows] * total
        mixed[rows] = (feature.astype(F32) + 5.0 * heat_ref[rows] + 12.5 * heat_two).astype(BF16)

    add_image(far, row_total, own_ref, other_ref, block_refs, held, lambda rows: sum_ref[rows], finish)
    half = keep_ref.shape[0]
    keep_ref[...] = mixed[pl.ds(pl.multiple_of(replica * half, half), half), :]
    send_ref[...] = mixed[pl.ds(pl.multiple_of((1 - replica) * half, half), half), :]


def project_kernel(keep_ref, got_ref, weight_ref, out_ref):
    replica = lax.axis_index("rep")
    part = keep_ref.shape[1]
    total = 0.0
    for mixed_ref, core in ((keep_ref, replica), (got_ref, 1 - replica)):
        weight = weight_ref[pl.ds(pl.multiple_of(core * part, part), part), :]
        total += jnp.dot(mixed_ref[...], weight, preferred_element_type=F32)
    out_ref[...] = total.astype(BF16)


def per_device(features, weight, tiles, tile_place, panel_count):
    rows_here, width = features.shape
    section_total = panel_count.shape[0]
    row_total = lax.axis_size("rows")
    rep_total = lax.axis_size("rep")
    half_rows = rows_here // rep_total
    part = width // rep_total
    shape = pltpu.VMEM
    panels = (section_total, rows_here, rows_here), BF16
    column = (rows_here, part), F32
    field = (rows_here, part), BF16
    held = (row_total, rows_here, part), BF16
    half = (half_rows, part), BF16

    dense, degree = pl.pallas_call(
        place_kernel,
        out_shape=(shape(*panels), shape(*column)),
        in_specs=[HBM, HBM, HBM],
        out_specs=(VMEM, VMEM),
        scratch_shapes=[
            pltpu.VMEM(tiles.shape, BF16),
            pltpu.SMEM(tile_place.shape, jnp.int32),
            pltpu.SMEM(panel_count.shape, jnp.int32),
            pltpu.SemaphoreType.DMA((section_total + 2,)),
        ],
        compiler_params=params(panels, panels, column),
    )(in_hbm(tile_place), in_hbm(panel_count), in_hbm(tiles))
    degree_other = swapped(degree, "rep")
    scale, first = pl.pallas_call(
        scale_kernel,
        out_shape=(shape(*column), shape(*field)),
        in_specs=[VMEM] * 3,
        out_specs=(VMEM, VMEM),
        compiler_params=params(column, column, column, column),
    )(degree, degree_other, features)

    dense_late, _ = lax.optimization_barrier((dense, scale))
    blocks, dense_other = gathered(first, "rows", row_total, swapped(dense_late, "rep"))
    dense_other = in_vmem(dense_other)

    def image(kernel, out_shape, blocks, *others, scratch=()):
        return pl.pallas_call(
            kernel,
            out_shape=out_shape,
            in_specs=[VMEM] * (2 + len(others) + len(blocks)),
            out_specs=jax.tree.map(lambda _: VMEM, out_shape),
            scratch_shapes=[pltpu.VMEM((len(blocks), rows_here, part), BF16), *scratch],
            compiler_params=params(panels, panels, column, column, column, held, held),
            cost_estimate=pl.CostEstimate(
                flops=2 * len(blocks) * rows_here * rows_here * part,
                bytes_accessed=0,
                transcendentals=0,
            ),
        )(dense, dense_other, *others, *blocks)

    cut = row_total // 2
    early = list(range(cut))
    arriving = [cut, *range(row_total - 1, cut, -1)]
    middle, late = arriving[: cut // 2], arriving[cut // 2 :]

    def image_start(blocks):
        total = image(
            functools.partial(near_kernel, early, row_total),
            shape(*column),
            [blocks[d] for d in early],
        )
        total = image(
            functools.partial(more_kernel, middle, row_total),
            shape(*column),
            [blocks[d] for d in middle],
            total,
        )
        return total, [blocks[d] for d in late]

    total, blocks = image_start(blocks)
    heat_one, second = image(
        functools.partial(first_kernel, late, row_total),
        (shape(*column), shape(*field)),
        blocks,
        total,
        scale,
    )
    total, blocks = image_start(gathered(second, "rows", row_total)[0])
    keep, send = image(
        functools.partial(second_kernel, late, row_total),
        (shape(*half), shape(*half)),
        blocks,
        total,
        scale,
        heat_one,
        features,
        scratch=[pltpu.VMEM(*field)],
    )
    got = swapped(send, "rep")
    return pl.pallas_call(
        project_kernel,
        out_shape=jax.ShapeDtypeStruct((half_rows, width), BF16),
        in_specs=[VMEM] * 3,
        out_specs=VMEM,
        compiler_params=params(column, column),
    )(keep, got, in_vmem(weight))


def solution(mesh):
    in_specs = (
        P(("groups", "rows"), None),
        P(),
        P(("groups", "rows", "rep"), None, None),
        P(("groups", "rows", "rep"), None),
        P(("groups", "rows", "rep")),
    )
    out_specs = P(("groups", "rows", "rep"), None)
    return jax.shard_map(
        per_device, mesh=mesh, in_specs=in_specs, out_specs=out_specs, check_vma=False
    )
```

```python
import functools
import math

import jax
import jax.numpy as jnp
from jax import lax
from jax.experimental import pallas as pl
from jax.experimental.pallas import tpu as pltpu
from jax.sharding import PartitionSpec as P

F32 = jnp.float32
BF16 = jnp.bfloat16
VMEM = pl.BlockSpec(memory_space=pltpu.VMEM)
HBM = pl.BlockSpec(memory_space=pltpu.HBM)


def params(*arrays):
    held = sum(math.prod(shape) * jnp.dtype(kind).itemsize for shape, kind in arrays)
    return pltpu.CompilerParams(vmem_limit_bytes=held + 6 * 2**20)


def in_vmem(block):
    return pltpu.with_memory_space_constraint(block, pltpu.VMEM)


def in_hbm(block):
    return pltpu.with_memory_space_constraint(block, pltpu.HBM)


def xor_permute(block, axis, distance):
    return lax.ppermute(block, axis, [(i, i ^ distance) for i in range(lax.axis_size(axis))])


def gathered(block, axis, size, also=None):
    half = size // 2
    blocks = {0: block}
    for d in [1, half, *range(2, half)]:
        blocks[d] = xor_permute(block, axis, d)
    early = [half, *range(1, half - 1)]
    tied, also = lax.optimization_barrier(([blocks[d] for d in early], also))
    blocks.update(zip(early, tied))
    for d in range(half - 1, 0, -1):
        blocks[half + d] = xor_permute(blocks[half], axis, d)
    return [blocks[d] for d in range(size)], also


def swapped(block, axis):
    return lax.ppermute(block, axis, [(0, 1), (1, 0)])


def place_kernel(
    place_hbm, count_hbm, tiles_ref, dense_ref, degree_ref, held, place_ref, count_ref, sems
):
    section_total, slot_total = place_ref.shape
    rows_here = dense_ref.shape[1]
    tile_dim = tiles_ref.shape[1]
    tile_span = rows_here // tile_dim

    def copy(s):
        slots = pl.ds(s * slot_total, slot_total)
        return pltpu.make_async_copy(tiles_ref.at[slots], held.at[slots], sems.at[s])

    places = pltpu.make_async_copy(place_hbm, place_ref, sems.at[section_total])
    counts = pltpu.make_async_copy(count_hbm, count_ref, sems.at[section_total + 1])
    places.start()
    counts.start()
    for s in range(section_total):
        copy(s).start()
    places.wait()
    counts.wait()
    for s in range(section_total):
        copy(s).wait()
        for k in range(slot_total):
            place = place_ref[s, k]
            row = pl.multiple_of((place // tile_span) * tile_dim, tile_dim)
            col = pl.multiple_of((place % tile_span) * tile_dim, tile_dim)
            tile = held[s * slot_total + k]
            dense_ref[s, pl.ds(row, tile_dim), pl.ds(col, tile_dim)] = jnp.where(
                k < count_ref[s], tile, jnp.zeros_like(tile)
            )
    ones = jnp.ones((rows_here, degree_ref.shape[1]), BF16)
    chunk = rows_here // 2
    for low in range(0, rows_here, chunk):
        rows = pl.ds(low, chunk)
        total = 0.0
        for s in range(section_total):
            total += jnp.dot(dense_ref[s, rows], ones, preferred_element_type=F32)
        degree_ref[rows] = total


def part_of(ref, index, size):
    return ref[:, pl.ds(pl.multiple_of(index * size, size), size)]


def scale_kernel(degree_ref, other_ref, feature_ref, scale_ref, first_ref):
    scale = lax.rsqrt(1.0 + (degree_ref[...] + other_ref[...]))
    scale_ref[...] = scale
    feature = part_of(feature_ref, lax.axis_index("rep"), scale.shape[1])
    first_ref[...] = (scale * feature.astype(F32)).astype(BF16)


def add_image(far, row_total, own_ref, other_ref, block_refs, held, start, finish, chunk=256):
    rep_total = row_total // own_ref.shape[0]
    row_index = lax.axis_index("rows")
    replica = lax.axis_index("rep")
    for i, block_ref in enumerate(block_refs):
        held[i] = block_ref[...]
    for first_row in range(0, own_ref.shape[1], chunk):
        rows = pl.ds(first_row, chunk)
        total = start(rows)
        for i in range(0, len(block_refs), rep_total):
            for dense_ref, core in ((own_ref, replica), (other_ref, 1 - replica)):
                column = row_index ^ (far[i] + core * (far[i + 1] - far[i]))
                section = lax.rem(row_index - column + row_total, row_total) // rep_total
                total += jnp.dot(
                    dense_ref[section, rows], held[i + core], preferred_element_type=F32
                )
        finish(rows, total)


def near_kernel(far, row_total, own_ref, other_ref, *refs):
    *block_refs, total_ref, held = refs

    def start(rows):
        return block_refs[0][rows].astype(F32)

    def finish(rows, total):
        total_ref[rows] = total

    add_image(far, row_total, own_ref, other_ref, block_refs, held, start, finish)


def more_kernel(far, row_total, own_ref, other_ref, sum_ref, *refs):
    *block_refs, total_ref, held = refs

    def finish(rows, total):
        total_ref[rows] = total

    add_image(far, row_total, own_ref, other_ref, block_refs, held, lambda rows: sum_ref[rows], finish)


def first_kernel(far, row_total, own_ref, other_ref, sum_ref, scale_ref, *refs):
    *block_refs, heat_ref, second_ref, held = refs

    def finish(rows, total):
        scale = scale_ref[rows]
        heat = scale * total
        heat_ref[rows] = heat
        second_ref[rows] = (scale * heat).astype(BF16)

    add_image(far, row_total, own_ref, other_ref, block_refs, held, lambda rows: sum_ref[rows], finish)


def second_kernel(
    far, row_total, own_ref, other_ref, sum_ref, scale_ref, heat_ref, feature_ref, *refs
):
    *block_refs, keep_ref, send_ref, held, mixed = refs
    replica = lax.axis_index("rep")
    part = mixed.shape[1]

    def finish(rows, total):
        feature = feature_ref[rows, pl.ds(pl.multiple_of(replica * part, part), part)]
        heat_two = scale_ref[rows] * total
        mixed[rows] = (feature.astype(F32) + 5.0 * heat_ref[rows] + 12.5 * heat_two).astype(BF16)

    add_image(far, row_total, own_ref, other_ref, block_refs, held, lambda rows: sum_ref[rows], finish)
    half = keep_ref.shape[0]
    keep_ref[...] = mixed[pl.ds(pl.multiple_of(replica * half, half), half), :]
    send_ref[...] = mixed[pl.ds(pl.multiple_of((1 - replica) * half, half), half), :]


def project_kernel(keep_ref, got_ref, weight_ref, out_ref):
    replica = lax.axis_index("rep")
    part = keep_ref.shape[1]
    total = 0.0
    for mixed_ref, core in ((keep_ref, replica), (got_ref, 1 - replica)):
        weight = weight_ref[pl.ds(pl.multiple_of(core * part, part), part), :]
        total += jnp.dot(mixed_ref[...], weight, preferred_element_type=F32)
    out_ref[...] = total.astype(BF16)


def per_device(features, weight, tiles, tile_place, panel_count):
    rows_here, width = features.shape
    section_total = panel_count.shape[0]
    row_total = lax.axis_size("rows")
    rep_total = lax.axis_size("rep")
    half_rows = rows_here // rep_total
    part = width // rep_total
    shape = pltpu.VMEM
    panels = (section_total, rows_here, rows_here), BF16
    column = (rows_here, part), F32
    field = (rows_here, part), BF16
    held = (row_total, rows_here, part), BF16
    half = (half_rows, part), BF16

    dense, degree = pl.pallas_call(
        place_kernel,
        out_shape=(shape(*panels), shape(*column)),
        in_specs=[HBM, HBM, HBM],
        out_specs=(VMEM, VMEM),
        scratch_shapes=[
            pltpu.VMEM(tiles.shape, BF16),
            pltpu.SMEM(tile_place.shape, jnp.int32),
            pltpu.SMEM(panel_count.shape, jnp.int32),
            pltpu.SemaphoreType.DMA((section_total + 2,)),
        ],
        compiler_params=params(panels, panels, column),
    )(in_hbm(tile_place), in_hbm(panel_count), in_hbm(tiles))
    degree_other = swapped(degree, "rep")
    scale, first = pl.pallas_call(
        scale_kernel,
        out_shape=(shape(*column), shape(*field)),
        in_specs=[VMEM] * 3,
        out_specs=(VMEM, VMEM),
        compiler_params=params(column, column, column, column),
    )(degree, degree_other, features)

    dense_late, _ = lax.optimization_barrier((dense, scale))
    blocks, _ = gathered(first, "rows", row_total)
    dense_other = swapped(dense_late, "rep")
    dense_other = in_vmem(dense_other)

    def image(kernel, out_shape, blocks, *others, scratch=()):
        return pl.pallas_call(
            kernel,
            out_shape=out_shape,
            in_specs=[VMEM] * (2 + len(others) + len(blocks)),
            out_specs=jax.tree.map(lambda _: VMEM, out_shape),
            scratch_shapes=[pltpu.VMEM((len(blocks), rows_here, part), BF16), *scratch],
            compiler_params=params(panels, panels, column, column, column, held, held),
            cost_estimate=pl.CostEstimate(
                flops=2 * len(blocks) * rows_here * rows_here * part,
                bytes_accessed=0,
                transcendentals=0,
            ),
        )(dense, dense_other, *others, *blocks)

    cut = row_total // 2
    early = list(range(cut))
    arriving = [cut, *range(row_total - 1, cut, -1)]
    middle, late = arriving[: cut // 2], arriving[cut // 2 :]

    def image_start(blocks):
        total = image(
            functools.partial(near_kernel, early, row_total),
            shape(*column),
            [blocks[d] for d in early],
        )
        total = image(
            functools.partial(more_kernel, middle, row_total),
            shape(*column),
            [blocks[d] for d in middle],
            total,
        )
        return total, [blocks[d] for d in late]

    total, blocks = image_start(blocks)
    heat_one, second = image(
        functools.partial(first_kernel, late, row_total),
        (shape(*column), shape(*field)),
        blocks,
        total,
        scale,
    )
    total, blocks = image_start(gathered(second, "rows", row_total)[0])
    keep, send = image(
        functools.partial(second_kernel, late, row_total),
        (shape(*half), shape(*half)),
        blocks,
        total,
        scale,
        heat_one,
        features,
        scratch=[pltpu.VMEM(*field)],
    )
    got = swapped(send, "rep")
    return pl.pallas_call(
        project_kernel,
        out_shape=jax.ShapeDtypeStruct((half_rows, width), BF16),
        in_specs=[VMEM] * 3,
        out_specs=VMEM,
        compiler_params=params(column, column),
    )(keep, got, in_vmem(weight))


def solution(mesh):
    in_specs = (
        P(("groups", "rows"), None),
        P(),
        P(("groups", "rows", "rep"), None, None),
        P(("groups", "rows", "rep"), None),
        P(("groups", "rows", "rep")),
    )
    out_specs = P(("groups", "rows", "rep"), None)
    return jax.shard_map(
        per_device, mesh=mesh, in_specs=in_specs, out_specs=out_specs, check_vma=False
    )
```

```python
import functools
import math

import jax
import jax.numpy as jnp
from jax import lax
from jax.experimental import pallas as pl
from jax.experimental.pallas import tpu as pltpu
from jax.sharding import PartitionSpec as P

F32 = jnp.float32
BF16 = jnp.bfloat16
VMEM = pl.BlockSpec(memory_space=pltpu.VMEM)
HBM = pl.BlockSpec(memory_space=pltpu.HBM)


def params(*arrays):
    held = sum(math.prod(shape) * jnp.dtype(kind).itemsize for shape, kind in arrays)
    return pltpu.CompilerParams(vmem_limit_bytes=held + 6 * 2**20)


def in_vmem(block):
    return pltpu.with_memory_space_constraint(block, pltpu.VMEM)


def in_hbm(block):
    return pltpu.with_memory_space_constraint(block, pltpu.HBM)


def xor_permute(block, axis, distance):
    return lax.ppermute(block, axis, [(i, i ^ distance) for i in range(lax.axis_size(axis))])


def gathered(block, axis, size, also=None):
    half = size // 2
    blocks = {0: block}
    for d in [1, half, *range(2, half)]:
        blocks[d] = xor_permute(block, axis, d)
    early = [half, *range(1, half - 1)]
    tied, also = lax.optimization_barrier(([blocks[d] for d in early], also))
    blocks.update(zip(early, tied))
    for d in range(half - 1, 0, -1):
        blocks[half + d] = xor_permute(blocks[half], axis, d)
    return [blocks[d] for d in range(size)], also


def swapped(block, axis):
    return lax.ppermute(block, axis, [(0, 1), (1, 0)])


def place_kernel(
    place_hbm, count_hbm, tiles_ref, dense_ref, degree_ref, held, place_ref, count_ref, sems
):
    section_total, slot_total = place_ref.shape
    rows_here = dense_ref.shape[1]
    tile_dim = tiles_ref.shape[1]
    tile_span = rows_here // tile_dim

    def copy(s):
        slots = pl.ds(s * slot_total, slot_total)
        return pltpu.make_async_copy(tiles_ref.at[slots], held.at[slots], sems.at[s])

    places = pltpu.make_async_copy(place_hbm, place_ref, sems.at[section_total])
    counts = pltpu.make_async_copy(count_hbm, count_ref, sems.at[section_total + 1])
    places.start()
    counts.start()
    for s in range(section_total):
        copy(s).start()
    places.wait()
    counts.wait()
    for s in range(section_total):
        copy(s).wait()
        for k in range(slot_total):
            place = place_ref[s, k]
            row = pl.multiple_of((place // tile_span) * tile_dim, tile_dim)
            col = pl.multiple_of((place % tile_span) * tile_dim, tile_dim)
            tile = held[s * slot_total + k]
            dense_ref[s, pl.ds(row, tile_dim), pl.ds(col, tile_dim)] = jnp.where(
                k < count_ref[s], tile, jnp.zeros_like(tile)
            )
    ones = jnp.ones((rows_here, tile_dim), BF16)
    chunk = rows_here // 2
    for low in range(0, rows_here, chunk):
        rows = pl.ds(low, chunk)
        total = 0.0
        for s in range(section_total):
            total += jnp.dot(dense_ref[s, rows], ones, preferred_element_type=F32)
        for i in range(chunk // tile_dim):
            square = total[i * tile_dim : (i + 1) * tile_dim]
            degree_ref[pl.ds(low // tile_dim + i, 1)] = square.T[:1]


def part_of(ref, index, size):
    return ref[:, pl.ds(pl.multiple_of(index * size, size), size)]


def scale_kernel(degree_ref, other_ref, feature_ref, scale_ref, first_ref):
    spans, side = degree_ref.shape
    row_scale = lax.rsqrt(1.0 + (degree_ref[...] + other_ref[...]))
    for i in range(spans):
        rows = pl.ds(i * side, side)
        scale = jnp.broadcast_to(row_scale[i : i + 1], (side, side)).T[:, : scale_ref.shape[1]]
        scale_ref[rows] = scale
        low = pl.multiple_of(lax.axis_index("rep") * side, side)
        feature = feature_ref[rows, pl.ds(low, side)]
        first_ref[rows] = (scale * feature.astype(F32)).astype(BF16)


def add_image(far, row_total, own_ref, other_ref, block_refs, held, start, finish, chunk=256):
    rep_total = row_total // own_ref.shape[0]
    row_index = lax.axis_index("rows")
    replica = lax.axis_index("rep")

    def product(rows, dense_ref, distance, block):
        column = row_index ^ distance
        section = lax.rem(row_index - column + row_total, row_total) // rep_total
        return jnp.dot(dense_ref[section, rows], block, preferred_element_type=F32)

    def run(single):
        for first_row in range(0, own_ref.shape[1], chunk):
            rows = pl.ds(first_row, chunk)
            total = start(rows)
            if single is not None:
                total += product(rows, single, far[0], block_refs[0][...])
            else:
                for i in range(0, len(block_refs), rep_total):
                    for dense_ref, core in ((own_ref, replica), (other_ref, 1 - replica)):
                        distance = far[i] + core * (far[i + 1] - far[i])
                        total += product(rows, dense_ref, distance, held[i + core])
            finish(rows, total)

    if len(far) > 1:
        for i, block_ref in enumerate(block_refs):
            held[i] = block_ref[...]
        run(None)
    else:
        pl.when(replica == far[0] % rep_total)(lambda: run(own_ref))
        pl.when(replica != far[0] % rep_total)(lambda: run(other_ref))


def near_kernel(far, row_total, own_ref, other_ref, *refs):
    *block_refs, total_ref, held = refs

    def start(rows):
        return block_refs[0][rows].astype(F32)

    def finish(rows, total):
        total_ref[rows] = total

    add_image(far, row_total, own_ref, other_ref, block_refs, held, start, finish)


def more_kernel(far, row_total, own_ref, other_ref, sum_ref, *refs):
    *block_refs, total_ref, held = refs

    def finish(rows, total):
        total_ref[rows] = total

    add_image(far, row_total, own_ref, other_ref, block_refs, held, lambda rows: sum_ref[rows], finish)


def first_kernel(far, row_total, own_ref, other_ref, sum_ref, scale_ref, *refs):
    *block_refs, heat_ref, second_ref, held = refs

    def finish(rows, total):
        scale = scale_ref[rows]
        heat = scale * total
        heat_ref[rows] = heat
        second_ref[rows] = (scale * heat).astype(BF16)

    add_image(far, row_total, own_ref, other_ref, block_refs, held, lambda rows: sum_ref[rows], finish)


def second_kernel(
    far, row_total, own_ref, other_ref, sum_ref, scale_ref, heat_ref, feature_ref, *refs
):
    *block_refs, keep_ref, send_ref, held, mixed = refs
    replica = lax.axis_index("rep")
    part = mixed.shape[1]

    def finish(rows, total):
        feature = feature_ref[rows, pl.ds(pl.multiple_of(replica * part, part), part)]
        heat_two = scale_ref[rows] * total
        mixed[rows] = (feature.astype(F32) + 5.0 * heat_ref[rows] + 12.5 * heat_two).astype(BF16)

    add_image(far, row_total, own_ref, other_ref, block_refs, held, lambda rows: sum_ref[rows], finish)
    half = keep_ref.shape[0]
    keep_ref[...] = mixed[pl.ds(pl.multiple_of(replica * half, half), half), :]
    send_ref[...] = mixed[pl.ds(pl.multiple_of((1 - replica) * half, half), half), :]


def project_kernel(keep_ref, got_ref, weight_ref, out_ref):
    replica = lax.axis_index("rep")
    part = keep_ref.shape[1]
    total = 0.0
    for mixed_ref, core in ((keep_ref, replica), (got_ref, 1 - replica)):
        weight = weight_ref[pl.ds(pl.multiple_of(core * part, part), part), :]
        total += jnp.dot(mixed_ref[...], weight, preferred_element_type=F32)
    out_ref[...] = total.astype(BF16)


def per_device(features, weight, tiles, tile_place, panel_count):
    rows_here, width = features.shape
    section_total = panel_count.shape[0]
    row_total = lax.axis_size("rows")
    rep_total = lax.axis_size("rep")
    half_rows = rows_here // rep_total
    part = width // rep_total
    shape = pltpu.VMEM
    panels = (section_total, rows_here, rows_here), BF16
    column = (rows_here, part), F32
    field = (rows_here, part), BF16
    held = (row_total, rows_here, part), BF16
    half = (half_rows, part), BF16

    dense, degree = pl.pallas_call(
        place_kernel,
        out_shape=(shape(*panels), shape((rows_here // tiles.shape[1], tiles.shape[1]), F32)),
        in_specs=[HBM, HBM, HBM],
        out_specs=(VMEM, VMEM),
        scratch_shapes=[
            pltpu.VMEM(tiles.shape, BF16),
            pltpu.SMEM(tile_place.shape, jnp.int32),
            pltpu.SMEM(panel_count.shape, jnp.int32),
            pltpu.SemaphoreType.DMA((section_total + 2,)),
        ],
        compiler_params=params(panels, panels, column),
    )(in_hbm(tile_place), in_hbm(panel_count), in_hbm(tiles))
    degree_other = swapped(degree, "rep")
    scale, first = pl.pallas_call(
        scale_kernel,
        out_shape=(shape(*column), shape(*field)),
        in_specs=[VMEM] * 3,
        out_specs=(VMEM, VMEM),
        compiler_params=params(column, column, column, column),
    )(degree, degree_other, features)

    dense_late, _ = lax.optimization_barrier((dense, scale))
    blocks, _ = gathered(first, "rows", row_total)
    dense_other = swapped(dense_late, "rep")
    dense_other = in_vmem(dense_other)

    def image(kernel, out_shape, blocks, *others, scratch=()):
        return pl.pallas_call(
            kernel,
            out_shape=out_shape,
            in_specs=[VMEM] * (2 + len(others) + len(blocks)),
            out_specs=jax.tree.map(lambda _: VMEM, out_shape),
            scratch_shapes=[pltpu.VMEM((len(blocks), rows_here, part), BF16), *scratch],
            compiler_params=params(panels, panels, column, column, column, held, held),
            cost_estimate=pl.CostEstimate(
                flops=2 * len(blocks) * rows_here * rows_here * part,
                bytes_accessed=0,
                transcendentals=0,
            ),
        )(dense, dense_other, *others, *blocks)

    cut = row_total // 2
    early = list(range(cut))
    arriving = [cut, *range(row_total - 1, cut, -1)]
    stages = [arriving[: cut // 2], *([d] for d in arriving[cut // 2 :])]
    late = stages.pop()

    def image_start(blocks):
        total = image(
            functools.partial(near_kernel, early, row_total),
            shape(*column),
            [blocks[d] for d in early],
        )
        for stage in stages:
            total = image(
                functools.partial(more_kernel, stage, row_total),
                shape(*column),
                [blocks[d] for d in stage],
                total,
            )
        return total, [blocks[d] for d in late]

    total, blocks = image_start(blocks)
    heat_one, second = image(
        functools.partial(first_kernel, late, row_total),
        (shape(*column), shape(*field)),
        blocks,
        total,
        scale,
    )
    total, blocks = image_start(gathered(second, "rows", row_total)[0])
    keep, send = image(
        functools.partial(second_kernel, late, row_total),
        (shape(*half), shape(*half)),
        blocks,
        total,
        scale,
        heat_one,
        features,
        scratch=[pltpu.VMEM(*field)],
    )
    got = swapped(send, "rep")
    return pl.pallas_call(
        project_kernel,
        out_shape=jax.ShapeDtypeStruct((half_rows, width), BF16),
        in_specs=[VMEM] * 3,
        out_specs=VMEM,
        compiler_params=params(column, column),
    )(keep, got, in_vmem(weight))


def solution(mesh):
    in_specs = (
        P(("groups", "rows"), None),
        P(),
        P(("groups", "rows", "rep"), None, None),
        P(("groups", "rows", "rep"), None),
        P(("groups", "rows", "rep")),
    )
    out_specs = P(("groups", "rows", "rep"), None)
    return jax.shard_map(
        per_device, mesh=mesh, in_specs=in_specs, out_specs=out_specs, check_vma=False
    )
```

```python
import functools
import math

import jax
import jax.numpy as jnp
from jax import lax
from jax.experimental import pallas as pl
from jax.experimental.pallas import tpu as pltpu
from jax.sharding import PartitionSpec as P

F32 = jnp.float32
BF16 = jnp.bfloat16
VMEM = pl.BlockSpec(memory_space=pltpu.VMEM)
HBM = pl.BlockSpec(memory_space=pltpu.HBM)


def params(*arrays):
    held = sum(math.prod(shape) * jnp.dtype(kind).itemsize for shape, kind in arrays)
    return pltpu.CompilerParams(vmem_limit_bytes=held + 6 * 2**20)


def in_vmem(block):
    return pltpu.with_memory_space_constraint(block, pltpu.VMEM)


def in_hbm(block):
    return pltpu.with_memory_space_constraint(block, pltpu.HBM)


def xor_permute(block, axis, distance):
    return lax.ppermute(block, axis, [(i, i ^ distance) for i in range(lax.axis_size(axis))])


def gathered(block, axis, size, also=None, far_last=False):
    half = size // 2
    blocks = {0: block}
    for d in [1, half, *range(2, half)]:
        blocks[d] = xor_permute(block, axis, d)
    near = range(1, half - 1)
    early = [*near[::-1], half] if far_last else [half, *near]
    tied, also = lax.optimization_barrier(([blocks[d] for d in early], also))
    blocks.update(zip(early, tied))
    for d in range(half - 1, 0, -1):
        blocks[half + d] = xor_permute(blocks[half], axis, d)
    return [blocks[d] for d in range(size)], also


def swapped(block, axis):
    return lax.ppermute(block, axis, [(0, 1), (1, 0)])


def place_kernel(
    place_hbm, count_hbm, tiles_ref, dense_ref, degree_ref, held, place_ref, count_ref, sems
):
    section_total, slot_total = place_ref.shape
    rows_here = dense_ref.shape[1]
    tile_dim = tiles_ref.shape[1]
    tile_span = rows_here // tile_dim

    def copy(s):
        slots = pl.ds(s * slot_total, slot_total)
        return pltpu.make_async_copy(tiles_ref.at[slots], held.at[slots], sems.at[s])

    places = pltpu.make_async_copy(place_hbm, place_ref, sems.at[section_total])
    counts = pltpu.make_async_copy(count_hbm, count_ref, sems.at[section_total + 1])
    places.start()
    counts.start()
    for s in range(section_total):
        copy(s).start()
    places.wait()
    counts.wait()
    for s in range(section_total):
        copy(s).wait()
        for k in range(slot_total):
            place = place_ref[s, k]
            row = pl.multiple_of((place // tile_span) * tile_dim, tile_dim)
            col = pl.multiple_of((place % tile_span) * tile_dim, tile_dim)
            tile = held[s * slot_total + k]
            dense_ref[s, pl.ds(row, tile_dim), pl.ds(col, tile_dim)] = jnp.where(
                k < count_ref[s], tile, jnp.zeros_like(tile)
            )
    ones = jnp.ones((rows_here, tile_dim), BF16)
    chunk = rows_here // 2
    for low in range(0, rows_here, chunk):
        rows = pl.ds(low, chunk)
        total = 0.0
        for s in range(section_total):
            total += jnp.dot(dense_ref[s, rows], ones, preferred_element_type=F32)
        for i in range(chunk // tile_dim):
            square = total[i * tile_dim : (i + 1) * tile_dim]
            degree_ref[pl.ds(low // tile_dim + i, 1)] = square.T[:1]


def part_of(ref, index, size):
    return ref[:, pl.ds(pl.multiple_of(index * size, size), size)]


def scale_kernel(degree_ref, other_ref, feature_ref, scale_ref, first_ref):
    spans, side = degree_ref.shape
    row_scale = lax.rsqrt(1.0 + (degree_ref[...] + other_ref[...]))
    for i in range(spans):
        rows = pl.ds(i * side, side)
        scale = jnp.broadcast_to(row_scale[i : i + 1], (side, side)).T[:, : scale_ref.shape[1]]
        scale_ref[rows] = scale
        low = pl.multiple_of(lax.axis_index("rep") * side, side)
        feature = feature_ref[rows, pl.ds(low, side)]
        first_ref[rows] = (scale * feature.astype(F32)).astype(BF16)


def add_image(far, row_total, own_ref, other_ref, block_refs, held, start, finish, lows=None, chunk=256):
    rep_total = row_total // own_ref.shape[0]
    row_index = lax.axis_index("rows")
    replica = lax.axis_index("rep")

    def product(rows, dense_ref, distance, block):
        column = row_index ^ distance
        section = lax.rem(row_index - column + row_total, row_total) // rep_total
        return jnp.dot(dense_ref[section, rows], block, preferred_element_type=F32)

    def run(single):
        for first_row in lows or range(0, own_ref.shape[1], chunk):
            rows = pl.ds(first_row, chunk)
            total = start(rows)
            if single is not None:
                total += product(rows, single, far[0], block_refs[0][...])
            else:
                for i in range(0, len(block_refs), rep_total):
                    for dense_ref, core in ((own_ref, replica), (other_ref, 1 - replica)):
                        distance = far[i] + core * (far[i + 1] - far[i])
                        total += product(rows, dense_ref, distance, held[i + core])
            finish(rows, total)

    if len(far) > 1:
        for i, block_ref in enumerate(block_refs):
            held[i] = block_ref[...]
        run(None)
    else:
        pl.when(replica == far[0] % rep_total)(lambda: run(own_ref))
        pl.when(replica != far[0] % rep_total)(lambda: run(other_ref))


def near_kernel(far, row_total, own_ref, other_ref, *refs):
    *block_refs, total_ref, held = refs

    def start(rows):
        return block_refs[0][rows].astype(F32)

    def finish(rows, total):
        total_ref[rows] = total

    add_image(far, row_total, own_ref, other_ref, block_refs, held, start, finish)


def more_kernel(far, row_total, own_ref, other_ref, sum_ref, *refs):
    *block_refs, total_ref, held = refs

    def finish(rows, total):
        total_ref[rows] = total

    add_image(far, row_total, own_ref, other_ref, block_refs, held, lambda rows: sum_ref[rows], finish)


def first_kernel(far, row_total, own_ref, other_ref, sum_ref, scale_ref, *refs):
    *block_refs, heat_ref, second_ref, held = refs

    def finish(rows, total):
        scale = scale_ref[rows]
        heat = scale * total
        heat_ref[rows] = heat
        second_ref[rows] = (scale * heat).astype(BF16)

    add_image(far, row_total, own_ref, other_ref, block_refs, held, lambda rows: sum_ref[rows], finish)


def mixed_half(far, row_total, core, refs, block_refs, held, put):
    own_ref, other_ref, sum_ref, scale_ref, heat_ref, feature_ref = refs
    half = own_ref.shape[1] // 2
    part = sum_ref.shape[1]
    low = pl.multiple_of(lax.axis_index("rep") * part, part)

    def finish(rows, total):
        feature = feature_ref[rows, pl.ds(low, part)]
        heat_two = scale_ref[rows] * total
        put((feature.astype(F32) + 5.0 * heat_ref[rows] + 12.5 * heat_two).astype(BF16))

    add_image(
        far,
        row_total,
        own_ref,
        other_ref,
        block_refs,
        held,
        lambda rows: sum_ref[rows],
        finish,
        [pl.multiple_of(core * half, half)],
        half,
    )


def send_kernel(far, row_total, *refs):
    *block_refs, send_ref, held = refs[6:]

    def put(mixed):
        send_ref[...] = mixed

    mixed_half(far, row_total, 1 - lax.axis_index("rep"), refs[:6], block_refs, held, put)


def keep_kernel(far, row_total, *refs):
    weight_ref, *block_refs, product_ref, held = refs[6:]
    replica = lax.axis_index("rep")
    part = block_refs[0].shape[1]

    def put(mixed):
        weight = weight_ref[pl.ds(pl.multiple_of(replica * part, part), part), :]
        product_ref[...] = jnp.dot(mixed, weight, preferred_element_type=F32)

    mixed_half(far, row_total, replica, refs[:6], block_refs, held, put)


def project_kernel(product_ref, got_ref, weight_ref, out_ref):
    part = got_ref.shape[1]
    low = pl.multiple_of((1 - lax.axis_index("rep")) * part, part)
    product = jnp.dot(got_ref[...], weight_ref[pl.ds(low, part), :], preferred_element_type=F32)
    out_ref[...] = (product_ref[...] + product).astype(BF16)


def per_device(features, weight, tiles, tile_place, panel_count):
    rows_here, width = features.shape
    section_total = panel_count.shape[0]
    row_total = lax.axis_size("rows")
    rep_total = lax.axis_size("rep")
    half_rows = rows_here // rep_total
    part = width // rep_total
    shape = pltpu.VMEM
    panels = (section_total, rows_here, rows_here), BF16
    column = (rows_here, part), F32
    field = (rows_here, part), BF16
    held = (row_total, rows_here, part), BF16
    half = (half_rows, part), BF16

    dense, degree = pl.pallas_call(
        place_kernel,
        out_shape=(shape(*panels), shape((rows_here // tiles.shape[1], tiles.shape[1]), F32)),
        in_specs=[HBM, HBM, HBM],
        out_specs=(VMEM, VMEM),
        scratch_shapes=[
            pltpu.VMEM(tiles.shape, BF16),
            pltpu.SMEM(tile_place.shape, jnp.int32),
            pltpu.SMEM(panel_count.shape, jnp.int32),
            pltpu.SemaphoreType.DMA((section_total + 2,)),
        ],
        compiler_params=params(panels, panels, column),
    )(in_hbm(tile_place), in_hbm(panel_count), in_hbm(tiles))
    degree_other = swapped(degree, "rep")
    scale, first = pl.pallas_call(
        scale_kernel,
        out_shape=(shape(*column), shape(*field)),
        in_specs=[VMEM] * 3,
        out_specs=(VMEM, VMEM),
        compiler_params=params(column, column, column, column),
    )(degree, degree_other, features)

    dense_late, _ = lax.optimization_barrier((dense, scale))
    blocks, _ = gathered(first, "rows", row_total, far_last=True)
    dense_other = swapped(dense_late, "rep")
    dense_other = in_vmem(dense_other)

    def image(kernel, out_shape, blocks, *others, scratch=()):
        return pl.pallas_call(
            kernel,
            out_shape=out_shape,
            in_specs=[VMEM] * (2 + len(others) + len(blocks)),
            out_specs=jax.tree.map(lambda _: VMEM, out_shape),
            scratch_shapes=[pltpu.VMEM((len(blocks), rows_here, part), BF16), *scratch],
            compiler_params=params(panels, panels, column, column, column, held, held),
            cost_estimate=pl.CostEstimate(
                flops=2 * len(blocks) * rows_here * rows_here * part,
                bytes_accessed=0,
                transcendentals=0,
            ),
        )(dense, dense_other, *others, *blocks)

    cut = row_total // 2
    early = list(range(cut))
    arriving = [cut, *range(row_total - 1, cut, -1)]
    stages = [arriving[: cut // 2], *([d] for d in arriving[cut // 2 :])]
    late = stages.pop()

    def image_start(blocks):
        total = image(
            functools.partial(near_kernel, early, row_total),
            shape(*column),
            [blocks[d] for d in early],
        )
        for stage in stages:
            total = image(
                functools.partial(more_kernel, stage, row_total),
                shape(*column),
                [blocks[d] for d in stage],
                total,
            )
        return total, [blocks[d] for d in late]

    total, blocks = image_start(blocks)
    heat_one, second = image(
        functools.partial(first_kernel, late, row_total),
        (shape(*column), shape(*field)),
        blocks,
        total,
        scale,
    )
    weight, second = lax.optimization_barrier((weight, second))
    total, blocks = image_start(gathered(second, "rows", row_total)[0])
    given = total, scale, heat_one, features
    send = image(functools.partial(send_kernel, late, row_total), shape(*half), blocks, *given)
    got = swapped(send, "rep")
    product = image(
        functools.partial(keep_kernel, late, row_total),
        shape((half_rows, width), F32),
        blocks,
        *given,
        in_vmem(weight),
    )
    return pl.pallas_call(
        project_kernel,
        out_shape=jax.ShapeDtypeStruct((half_rows, width), BF16),
        in_specs=[VMEM] * 3,
        out_specs=VMEM,
        compiler_params=params(column, column),
    )(product, got, in_vmem(weight))


def solution(mesh):
    in_specs = (
        P(("groups", "rows"), None),
        P(),
        P(("groups", "rows", "rep"), None, None),
        P(("groups", "rows", "rep"), None),
        P(("groups", "rows", "rep")),
    )
    out_specs = P(("groups", "rows", "rep"), None)
    return jax.shard_map(
        per_device, mesh=mesh, in_specs=in_specs, out_specs=out_specs, check_vma=False
    )
```

```python
import functools
import math

import jax
import jax.numpy as jnp
from jax import lax
from jax.experimental import pallas as pl
from jax.experimental.pallas import tpu as pltpu
from jax.sharding import PartitionSpec as P

F32 = jnp.float32
BF16 = jnp.bfloat16
VMEM = pl.BlockSpec(memory_space=pltpu.VMEM)
HBM = pl.BlockSpec(memory_space=pltpu.HBM)


def params(*arrays):
    held = sum(math.prod(shape) * jnp.dtype(kind).itemsize for shape, kind in arrays)
    return pltpu.CompilerParams(vmem_limit_bytes=held + 6 * 2**20)


def in_vmem(block):
    return pltpu.with_memory_space_constraint(block, pltpu.VMEM)


def in_hbm(block):
    return pltpu.with_memory_space_constraint(block, pltpu.HBM)


def xor_permute(block, axis, distance):
    return lax.ppermute(block, axis, [(i, i ^ distance) for i in range(lax.axis_size(axis))])


def gathered(block, axis, size, also=None, far_last=False):
    half = size // 2
    blocks = {0: block}
    for d in [1, half, *range(2, half)]:
        blocks[d] = xor_permute(block, axis, d)
    near = range(1, half - 1)
    early = [*near[::-1], half] if far_last else [half, *near[::-1]]
    tied, also = lax.optimization_barrier(([blocks[d] for d in early], also))
    blocks.update(zip(early, tied))
    for d in range(half - 1, 0, -1):
        blocks[half + d] = xor_permute(blocks[half], axis, d)
    return [blocks[d] for d in range(size)], also


def swapped(block, axis):
    return lax.ppermute(block, axis, [(0, 1), (1, 0)])


def place_kernel(
    place_hbm, count_hbm, tiles_ref, dense_ref, degree_ref, held, place_ref, count_ref, sems
):
    section_total, slot_total = place_ref.shape
    rows_here = dense_ref.shape[1]
    tile_dim = tiles_ref.shape[1]
    tile_span = rows_here // tile_dim

    def copy(s):
        slots = pl.ds(s * slot_total, slot_total)
        return pltpu.make_async_copy(tiles_ref.at[slots], held.at[slots], sems.at[s])

    places = pltpu.make_async_copy(place_hbm, place_ref, sems.at[section_total])
    counts = pltpu.make_async_copy(count_hbm, count_ref, sems.at[section_total + 1])
    places.start()
    counts.start()
    for s in range(section_total):
        copy(s).start()
    places.wait()
    counts.wait()
    for s in range(section_total):
        copy(s).wait()
        for k in range(slot_total):
            place = place_ref[s, k]
            row = pl.multiple_of((place // tile_span) * tile_dim, tile_dim)
            col = pl.multiple_of((place % tile_span) * tile_dim, tile_dim)
            tile = held[s * slot_total + k]
            dense_ref[s, pl.ds(row, tile_dim), pl.ds(col, tile_dim)] = jnp.where(
                k < count_ref[s], tile, jnp.zeros_like(tile)
            )
    ones = jnp.ones((rows_here, tile_dim), BF16)
    chunk = rows_here // 2
    for low in range(0, rows_here, chunk):
        rows = pl.ds(low, chunk)
        total = 0.0
        for s in range(section_total):
            total += jnp.dot(dense_ref[s, rows], ones, preferred_element_type=F32)
        for i in range(chunk // tile_dim):
            square = total[i * tile_dim : (i + 1) * tile_dim]
            degree_ref[pl.ds(low // tile_dim + i, 1)] = square.T[:1]


def part_of(ref, index, size):
    return ref[:, pl.ds(pl.multiple_of(index * size, size), size)]


def scale_kernel(degree_ref, other_ref, feature_ref, scale_ref, first_ref):
    spans, side = degree_ref.shape
    row_scale = lax.rsqrt(1.0 + (degree_ref[...] + other_ref[...]))
    for i in range(spans):
        rows = pl.ds(i * side, side)
        scale = jnp.broadcast_to(row_scale[i : i + 1], (side, side)).T[:, : scale_ref.shape[1]]
        scale_ref[rows] = scale
        low = pl.multiple_of(lax.axis_index("rep") * side, side)
        feature = feature_ref[rows, pl.ds(low, side)]
        first_ref[rows] = (scale * feature.astype(F32)).astype(BF16)


def add_image(far, row_total, own_ref, other_ref, block_refs, held, start, finish, lows=None, chunk=256):
    rep_total = row_total // own_ref.shape[0]
    row_index = lax.axis_index("rows")
    replica = lax.axis_index("rep")

    def product(rows, dense_ref, distance, block):
        column = row_index ^ distance
        section = lax.rem(row_index - column + row_total, row_total) // rep_total
        return jnp.dot(dense_ref[section, rows], block, preferred_element_type=F32)

    def run(single):
        for first_row in lows or range(0, own_ref.shape[1], chunk):
            rows = pl.ds(first_row, chunk)
            total = start(rows)
            if single is not None:
                total += product(rows, single, far[0], block_refs[0][...])
            else:
                for i in range(0, len(block_refs), rep_total):
                    for dense_ref, core in ((own_ref, replica), (other_ref, 1 - replica)):
                        distance = far[i] + core * (far[i + 1] - far[i])
                        total += product(rows, dense_ref, distance, held[i + core])
            finish(rows, total)

    if len(far) > 1:
        for i, block_ref in enumerate(block_refs):
            held[i] = block_ref[...]
        run(None)
    else:
        pl.when(replica == far[0] % rep_total)(lambda: run(own_ref))
        pl.when(replica != far[0] % rep_total)(lambda: run(other_ref))


def near_kernel(far, row_total, own_ref, other_ref, *refs):
    *block_refs, total_ref, held = refs

    def start(rows):
        return block_refs[0][rows].astype(F32)

    def finish(rows, total):
        total_ref[rows] = total

    add_image(far, row_total, own_ref, other_ref, block_refs, held, start, finish)


def more_kernel(far, row_total, own_ref, other_ref, sum_ref, *refs):
    *block_refs, total_ref, held = refs

    def finish(rows, total):
        total_ref[rows] = total

    add_image(far, row_total, own_ref, other_ref, block_refs, held, lambda rows: sum_ref[rows], finish)


def first_kernel(far, row_total, own_ref, other_ref, sum_ref, scale_ref, *refs):
    *block_refs, heat_ref, second_ref, held = refs

    def finish(rows, total):
        scale = scale_ref[rows]
        heat = scale * total
        heat_ref[rows] = heat
        second_ref[rows] = (scale * heat).astype(BF16)

    add_image(far, row_total, own_ref, other_ref, block_refs, held, lambda rows: sum_ref[rows], finish)


def mixed_half(far, row_total, core, refs, block_refs, held, put):
    own_ref, other_ref, sum_ref, scale_ref, heat_ref, feature_ref = refs
    half = own_ref.shape[1] // 2
    part = sum_ref.shape[1]
    low = pl.multiple_of(lax.axis_index("rep") * part, part)

    def finish(rows, total):
        feature = feature_ref[rows, pl.ds(low, part)]
        heat_two = scale_ref[rows] * total
        put((feature.astype(F32) + 5.0 * heat_ref[rows] + 12.5 * heat_two).astype(BF16))

    add_image(
        far,
        row_total,
        own_ref,
        other_ref,
        block_refs,
        held,
        lambda rows: sum_ref[rows],
        finish,
        [pl.multiple_of(core * half, half)],
        half,
    )


def send_kernel(far, row_total, *refs):
    *block_refs, send_ref, held = refs[6:]

    def put(mixed):
        send_ref[...] = mixed

    mixed_half(far, row_total, 1 - lax.axis_index("rep"), refs[:6], block_refs, held, put)


def keep_kernel(far, row_total, *refs):
    weight_ref, *block_refs, product_ref, held = refs[6:]
    replica = lax.axis_index("rep")
    part = block_refs[0].shape[1]

    def put(mixed):
        weight = weight_ref[pl.ds(pl.multiple_of(replica * part, part), part), :]
        product_ref[...] = jnp.dot(mixed, weight, preferred_element_type=F32)

    mixed_half(far, row_total, replica, refs[:6], block_refs, held, put)


def project_kernel(product_ref, got_ref, weight_ref, out_ref):
    part = got_ref.shape[1]
    low = pl.multiple_of((1 - lax.axis_index("rep")) * part, part)
    product = jnp.dot(got_ref[...], weight_ref[pl.ds(low, part), :], preferred_element_type=F32)
    out_ref[...] = (product_ref[...] + product).astype(BF16)


def per_device(features, weight, tiles, tile_place, panel_count):
    rows_here, width = features.shape
    section_total = panel_count.shape[0]
    row_total = lax.axis_size("rows")
    rep_total = lax.axis_size("rep")
    half_rows = rows_here // rep_total
    part = width // rep_total
    shape = pltpu.VMEM
    panels = (section_total, rows_here, rows_here), BF16
    column = (rows_here, part), F32
    field = (rows_here, part), BF16
    held = (row_total, rows_here, part), BF16
    half = (half_rows, part), BF16

    dense, degree = pl.pallas_call(
        place_kernel,
        out_shape=(shape(*panels), shape((rows_here // tiles.shape[1], tiles.shape[1]), F32)),
        in_specs=[HBM, HBM, HBM],
        out_specs=(VMEM, VMEM),
        scratch_shapes=[
            pltpu.VMEM(tiles.shape, BF16),
            pltpu.SMEM(tile_place.shape, jnp.int32),
            pltpu.SMEM(panel_count.shape, jnp.int32),
            pltpu.SemaphoreType.DMA((section_total + 2,)),
        ],
        compiler_params=params(panels, panels, column),
    )(in_hbm(tile_place), in_hbm(panel_count), in_hbm(tiles))
    degree_other = swapped(degree, "rep")
    scale, first = pl.pallas_call(
        scale_kernel,
        out_shape=(shape(*column), shape(*field)),
        in_specs=[VMEM] * 3,
        out_specs=(VMEM, VMEM),
        compiler_params=params(column, column, column, column),
    )(degree, degree_other, features)

    dense_late, _ = lax.optimization_barrier((dense, scale))
    blocks, _ = gathered(first, "rows", row_total, far_last=True)
    dense_other = swapped(dense_late, "rep")
    dense_other = in_vmem(dense_other)

    def image(kernel, out_shape, blocks, *others, scratch=()):
        return pl.pallas_call(
            kernel,
            out_shape=out_shape,
            in_specs=[VMEM] * (2 + len(others) + len(blocks)),
            out_specs=jax.tree.map(lambda _: VMEM, out_shape),
            scratch_shapes=[pltpu.VMEM((len(blocks), rows_here, part), BF16), *scratch],
            compiler_params=params(panels, panels, column, column, column, held, held),
            cost_estimate=pl.CostEstimate(
                flops=2 * len(blocks) * rows_here * rows_here * part,
                bytes_accessed=0,
                transcendentals=0,
            ),
        )(dense, dense_other, *others, *blocks)

    cut = row_total // 2
    early = list(range(cut))
    arriving = [cut, *range(row_total - 1, cut, -1)]
    stages = [arriving[: cut // 2], *([d] for d in arriving[cut // 2 :])]
    late = stages.pop()

    def image_start(blocks):
        total = image(
            functools.partial(near_kernel, early, row_total),
            shape(*column),
            [blocks[d] for d in early],
        )
        for stage in stages:
            total = image(
                functools.partial(more_kernel, stage, row_total),
                shape(*column),
                [blocks[d] for d in stage],
                total,
            )
        return total, [blocks[d] for d in late]

    total, blocks = image_start(blocks)
    heat_one, second = image(
        functools.partial(first_kernel, late, row_total),
        (shape(*column), shape(*field)),
        blocks,
        total,
        scale,
    )
    weight, second = lax.optimization_barrier((weight, second))
    total, blocks = image_start(gathered(second, "rows", row_total)[0])
    given = total, scale, heat_one, features
    send = image(functools.partial(send_kernel, late, row_total), shape(*half), blocks, *given)
    got = swapped(send, "rep")
    product = image(
        functools.partial(keep_kernel, late, row_total),
        shape((half_rows, width), F32),
        blocks,
        *given,
        in_vmem(weight),
    )
    return pl.pallas_call(
        project_kernel,
        out_shape=jax.ShapeDtypeStruct((half_rows, width), BF16),
        in_specs=[VMEM] * 3,
        out_specs=VMEM,
        compiler_params=params(column, column),
    )(product, got, in_vmem(weight))


def solution(mesh):
    in_specs = (
        P(("groups", "rows"), None),
        P(),
        P(("groups", "rows", "rep"), None, None),
        P(("groups", "rows", "rep"), None),
        P(("groups", "rows", "rep")),
    )
    out_specs = P(("groups", "rows", "rep"), None)
    return jax.shard_map(
        per_device, mesh=mesh, in_specs=in_specs, out_specs=out_specs, check_vma=False
    )
```
